128 devices in a mesh: row: 8 (over y, core), col: 16 (over x, z).
Axes of the slice: x: 4, y: 4, z: 4, core: 2. Of those that a mesh axis runs over, the one named last changes fastest.
Arguments:
- inputs: bfloat16 [1024, 12288], P('col', 'row'), may hold values from -6 to 6
- pre_act: bfloat16 [1024, 24576], P('row', 'col'), may hold values from -6 to 6
- out_grad: bfloat16 [1024, 12288], P('col', 'row'), may hold values from -6 to 6
- up_payload: bfloat16 [12288, 24576], P('row', 'col'), may hold values from -15 to 15, as said below
- up_scale: int32 [384, 24576], P('row', 'col'), may hold values from -10 to -8
- down_payload: bfloat16 [24576, 12288], P('col', 'row'), may hold values from -15 to 15, as said below
- down_scale: int32 [768, 12288], P('col', 'row'), may hold values from -11 to -9
Outputs:
- input_grad: bfloat16 [1024, 12288], P('col', 'row')
- up_grad: bfloat16 [12288, 24576], P('row', 'col')
- down_grad: bfloat16 [24576, 12288], P('col', 'row')
The draws below stay inside these ranges and needn't reach their ends.
Inputs may be any that keep to these rules, and one draw needn't show every extreme that they name: `up_payload`: each entry is an FP8 E4M3 number: a sign times (1 + m / 8) times 2 ** e, m from 0 to 7, e from 0 to 3. `down_payload`: each entry is an FP8 E4M3 number: a sign times (1 + m / 8) times 2 ** e, m from 0 to 7, e from 0 to 3.
All inputs are finite; a program needn't handle non-finite values.
Results may differ from the reference program's by a relative error of at most 0.005.
Values may be sent and summed in bfloat16 or wider, within the bound.
No kernel may reach another device: no remote copies, remote signals or barrier semaphores. Data moves between devices by JAX's collectives and lax.ppermute only.
A program may use at most 128 MiB of HBM per device.

```python
import jax
import jax.numpy as jnp
from jax import lax

D = 12288
F = 24576
TOKENS = 1024


def fp8_values(key, dims_shape, exp_top):
    key_sign, key_mantissa, key_exponent = jax.random.split(key, 3)
    sign_bits = jax.random.randint(key_sign, dims_shape, 0, 2) * 2 - 1
    mantissa = jax.random.randint(key_mantissa, dims_shape, 0, 8)
    exponent = jax.random.randint(key_exponent, dims_shape, 0, exp_top)
    values = sign_bits.astype(jnp.float32) * (1.0 + mantissa.astype(jnp.float32) / 8.0) * jnp.exp2(exponent.astype(jnp.float32))
    return values.astype(jnp.bfloat16)


def draw_up_payload(key, part):
    key = jax.random.fold_in(key, 11)
    exp_top = 3
    return fp8_values(key, (D, F), exp_top)


def draw_down_payload(key, part):
    key = jax.random.fold_in(key, 23)
    exp_top = 3
    return fp8_values(key, (F, D), exp_top)


def plant(values, own_key, smallest, largest):
    longest = values.shape.index(max(values.shape))
    spots = []
    for shift in (0, 1):
        where = [jax.random.randint(jax.random.fold_in(own_key, axis), (), 0, length) for axis, length in enumerate(values.shape)]
        where[longest] = (where[longest] + shift) % values.shape[longest]
        spots.append(tuple(where))
    return values.at[spots[0]].set(smallest).at[spots[1]].set(largest)


def levels(rng, extent, shards, low, top_value):
    factor_of, own = 1.0, jax.random.fold_in(rng, 6)
    for axis_at, parts in shards:
        steps = jnp.exp(jax.random.uniform(jax.random.fold_in(own, axis_at), (parts,), jnp.float32, low / len(shards), top_value / len(shards)))
        factor_of = factor_of * jnp.repeat(steps, extent[axis_at] // parts).reshape([-1 if axis == axis_at else 1 for axis in range(len(extent))])
    return factor_of


def centred(rng, shape, spread, reach, cuts=(), dtype=jnp.bfloat16):
    values = spread * jax.random.normal(rng, shape, jnp.float32)
    if cuts:
        values = values * levels(rng, shape, cuts, -0.22, 0.18)
    return jnp.clip(values, -reach, reach).astype(dtype)


def setup_inputs(seed: int = 0) -> dict:
    streams_of = jax.random.split(jax.random.key(seed), 8)
    inputs = centred(streams_of[0], (TOKENS, D), 1.0, 6.0, ((0, 16), (1, 8)))
    pre_act = centred(streams_of[1], (TOKENS, F), 1.0, 6.0, ((0, 8), (1, 16)))
    out_grad = centred(streams_of[2], (TOKENS, D), 1.0, 6.0, ((0, 16), (1, 8)))
    up_payload = draw_up_payload(jax.random.fold_in(streams_of[7], 71), 0)
    up_scale = plant(jax.random.randint(streams_of[4], (D // 32, F), -10, -7), jax.random.fold_in(streams_of[4], 1), -10, (-7) - 1).astype(jnp.int32)
    down_payload = draw_down_payload(jax.random.fold_in(streams_of[7], 71), 0)
    down_scale = plant(jax.random.randint(streams_of[6], (F // 32, D), -11, -8), jax.random.fold_in(streams_of[6], 1), -11, (-8) - 1).astype(jnp.int32)
    return dict(inputs=inputs, pre_act=pre_act, out_grad=out_grad, up_payload=up_payload, up_scale=up_scale, down_payload=down_payload, down_scale=down_scale)


def dequantize(payload, scale):
    rows, cols = payload.shape
    blocks = payload.astype(jnp.float32).reshape(rows // 32, 32, cols)
    factor = jnp.exp2(scale.astype(jnp.float32))[:, None, :]
    return (blocks * factor).reshape(rows, cols).astype(jnp.bfloat16)


def gelu_terms(pre):
    values = pre.astype(jnp.float32)
    normal_cdf = 0.5 * (1.0 + jax.scipy.special.erf(values * 0.7071067811865476))
    activated = values * normal_cdf
    gelu_slope = normal_cdf + values * jnp.exp(-0.5 * values * values) * 0.3989422804014327
    return activated, gelu_slope


def reference(inputs, pre_act, out_grad, up_payload, up_scale, down_payload, down_scale):
    up_weight = dequantize(up_payload, up_scale)
    down_weight = dequantize(down_payload, down_scale)
    hidden_grad = lax.dot_general(out_grad, down_weight, (((1,), (1,)), ((), ())), preferred_element_type=jnp.float32)
    activated, gelu_slope = gelu_terms(pre_act)
    activated = activated.astype(jnp.bfloat16)
    gated_grad = (gelu_slope * hidden_grad).astype(jnp.bfloat16)
    down_grad = lax.dot_general(activated, out_grad, (((0,), (0,)), ((), ())), preferred_element_type=jnp.float32).astype(jnp.bfloat16)
    up_grad = lax.dot_general(inputs, gated_grad, (((0,), (0,)), ((), ())), preferred_element_type=jnp.float32).astype(jnp.bfloat16)
    input_grad = lax.dot_general(gated_grad, up_weight, (((1,), (1,)), ((), ())), preferred_element_type=jnp.float32).astype(jnp.bfloat16)
    return input_grad, up_grad, down_grad
```

```python
import jax
import jax.numpy as jnp
from jax import lax
from jax.experimental import pallas as pl
from jax.experimental.pallas import tpu as pltpu
from jax.sharding import Mesh
from jax.sharding import PartitionSpec as P

BF16, F32 = jnp.bfloat16, jnp.float32
TILE = 256


def dequantize(payload, scale):
    rows, cols = payload.shape
    blocks = payload.astype(F32).reshape(rows // 32, 32, cols)
    factor = jnp.exp2(scale.astype(F32))[:, None, :]
    return (blocks * factor).reshape(rows, cols).astype(BF16)


def gelu_terms(pre):
    values = pre.astype(F32)
    normal_cdf = 0.5 * (1.0 + jax.scipy.special.erf(values * 0.7071067811865476))
    activated = values * normal_cdf
    gelu_slope = normal_cdf + values * jnp.exp(-0.5 * values * values) * 0.3989422804014327
    return (activated, gelu_slope)


def shift_grid(first, step):
    pairs = []
    for k in range(2):
        for x in range(4):
            for z in range(4):
                along_x = (k == 0) == first
                to = (k, (x - step) % 4, z) if along_x else (k, x, (z - step) % 4)
                pairs.append((k * 16 + x * 4 + z, to[0] * 16 + to[1] * 4 + to[2]))
    return pairs


def from_grid(value, first, step):
    return lax.ppermute(value, ("k", "x", "z"), shift_grid(first, step))


def from_y(value, step):
    return lax.ppermute(value, "y", [(i, (i - step) % 4) for i in range(4)])


def swap_cores(value):
    return lax.ppermute(value, "k", [(0, 1), (1, 0)])


def gather_grid(block):
    stage = jnp.concatenate([block] + [from_grid(block, True, step) for step in (1, 2, 3)])
    return [stage] + [from_grid(stage, False, step) for step in (1, 2, 3)]


def gather_y(block):
    own = jnp.concatenate([block] + [from_y(block, step) for step in (1, 2, 3)])
    return own, swap_cores(own)


def place_of(x, z):
    k, y = lax.axis_index("k"), lax.axis_index("y")
    half = lax.rem(z // 2 + k, 2)
    return half * 8 + lax.rem(x - y + 4, 4) * 2 + lax.rem(z, 2)


def grid_position(i, j):
    k, x, z = lax.axis_index("k"), lax.axis_index("x"), lax.axis_index("z")
    x = lax.rem(x + jnp.where(k == 0, i, j), 4)
    z = lax.rem(z + jnp.where(k == 0, j, i), 4)
    return x, z


def collect(pieces, held, sems):
    copies = []
    for j in range(4):
        for i in range(4):
            place = place_of(*grid_position(i, j))
            rows = pl.ds(pl.multiple_of(place * 64, 64), 64)
            copies.append(
                pltpu.make_async_copy(pieces[j].at[pl.ds(i * 64, 64)], held.at[rows], sems.at[j * 4 + i])
            )
    for copy in copies:
        copy.start()
    for copy in copies:
        copy.wait()


NT = (((1,), (1,)), ((), ()))
TN = (((0,), (0,)), ((), ()))
ANY = pl.BlockSpec(memory_space=pl.ANY)


def params():
    return pltpu.CompilerParams(vmem_limit_bytes=32 * 1024 * 1024)


def cost(flops, moved):
    return pl.CostEstimate(flops=flops, bytes_accessed=moved, transcendentals=0)


def hidden_kernel(p0, p1, p2, p3, w, other, own, held, sems):
    @pl.when(pl.program_id(0) == 0)
    def _():
        collect([p0, p1, p2, p3], held, sems)

    weight = w[...]
    own[...] = lax.dot_general(held[:512], weight, NT, preferred_element_type=F32)
    other[...] = lax.dot_general(held[512:], weight, NT, preferred_element_type=F32).astype(BF16)


def hidden_partial(pieces, weight):
    n, depth = weight.shape
    return pl.pallas_call(
        hidden_kernel,
        grid=(n // TILE,),
        out_shape=(jax.ShapeDtypeStruct((512, n), BF16), jax.ShapeDtypeStruct((512, n), F32)),
        in_specs=[ANY] * 4 + [pl.BlockSpec((TILE, depth), lambda i: (i, 0))],
        out_specs=[pl.BlockSpec((512, TILE), lambda i: (0, i))] * 2,
        scratch_shapes=[pltpu.VMEM((1024, depth), BF16), pltpu.SemaphoreType.DMA((16,))],
        compiler_params=params(),
        cost_estimate=cost(2 * 1024 * n * depth, 2 * (1024 + n) * depth + 6 * 512 * n),
        name="hidden_partial",
    )(*pieces, weight)


def input_kernel(mine, theirs, w, o0, o1, o2, o3, held, sems):
    @pl.when(pl.program_id(0) == 0)
    def _():
        copies = []
        for j in range(4):
            for i in range(4):
                place = place_of(*grid_position(i, j))
                rows = pl.ds(pl.multiple_of(lax.rem(place, 8) * 64, 64), 64)
                to = held.at[pl.ds(i * 256 + j * 64, 64)]
                sem = sems.at[i * 4 + j]
                here = pltpu.make_async_copy(mine.at[rows], to, sem)
                there = pltpu.make_async_copy(theirs.at[rows], to, sem)
                pl.when(place < 8)(here.start)
                pl.when(place >= 8)(there.start)
                copies.append(here)
        for copy in copies:
            copy.wait()

    out = lax.dot_general(held[...], w[...], NT, preferred_element_type=F32)
    o0[...] = out[:256]
    o1[...] = out[256:512].astype(BF16)
    o2[...] = out[512:768].astype(BF16)
    o3[...] = out[768:].astype(BF16)


def input_partial(mine, theirs, weight):
    n, depth = weight.shape
    return pl.pallas_call(
        input_kernel,
        grid=(n // TILE,),
        out_shape=[jax.ShapeDtypeStruct((256, n), F32)] + [jax.ShapeDtypeStruct((256, n), BF16)] * 3,
        in_specs=[ANY] * 2 + [pl.BlockSpec((TILE, depth), lambda i: (i, 0))],
        out_specs=[pl.BlockSpec((256, TILE), lambda i: (0, i))] * 4,
        scratch_shapes=[pltpu.VMEM((1024, depth), BF16), pltpu.SemaphoreType.DMA((16,))],
        compiler_params=params(),
        cost_estimate=cost(2 * 1024 * n * depth, 2 * (1024 + n) * depth + 10 * 256 * n),
        name="input_partial",
    )(mine, theirs, weight)


def down_kernel(mine, theirs, p0, p1, p2, p3, out, held, sems):
    @pl.when(pl.program_id(0) == 0)
    def _():
        collect([p0, p1, p2, p3], held, sems)

    total = lax.dot_general(mine[...], held[:512], TN, preferred_element_type=F32)
    total += lax.dot_general(theirs[...], held[512:], TN, preferred_element_type=F32)
    out[...] = total.astype(BF16)


def down_gradient(mine, theirs, pieces):
    m, n = mine.shape[1], pieces[0].shape[1]
    return pl.pallas_call(
        down_kernel,
        grid=(m // TILE,),
        out_shape=jax.ShapeDtypeStruct((m, n), BF16),
        in_specs=[pl.BlockSpec((512, TILE), lambda i: (0, i))] * 2 + [ANY] * 4,
        out_specs=pl.BlockSpec((TILE, n), lambda i: (i, 0)),
        scratch_shapes=[pltpu.VMEM((1024, n), BF16), pltpu.SemaphoreType.DMA((16,))],
        compiler_params=params(),
        cost_estimate=cost(2 * 1024 * n * m, 2 * 1024 * (n + m) + 2 * n * m),
        name="down_gradient",
    )(mine, theirs, *pieces)


def up_kernel(mine, theirs, p0, p1, p2, p3, out, held, sems):
    @pl.when(pl.program_id(0) == 0)
    def _():
        collect([p0, p1, p2, p3], held, sems)

    columns = pl.ds(pl.multiple_of(pl.program_id(0) * TILE, TILE), TILE)
    total = lax.dot_general(held[:512, columns], mine[...], TN, preferred_element_type=F32)
    total += lax.dot_general(held[512:, columns], theirs[...], TN, preferred_element_type=F32)
    out[...] = total.astype(BF16)


def up_gradient(mine, theirs, pieces):
    m, n = pieces[0].shape[1], mine.shape[1]
    return pl.pallas_call(
        up_kernel,
        grid=(m // TILE,),
        out_shape=jax.ShapeDtypeStruct((m, n), BF16),
        in_specs=[pl.BlockSpec((512, n), lambda i: (0, 0))] * 2 + [ANY] * 4,
        out_specs=pl.BlockSpec((TILE, n), lambda i: (i, 0)),
        scratch_shapes=[pltpu.VMEM((1024, m), BF16), pltpu.SemaphoreType.DMA((16,))],
        compiler_params=params(),
        cost_estimate=cost(2 * 1024 * n * m, 2 * 1024 * (n + m) + 2 * n * m),
        name="up_gradient",
    )(mine, theirs, *pieces)


def per_device(inputs, pre_act, out_grad, up_payload, up_scale, down_payload, down_scale):
    grad_pieces = gather_grid(out_grad)
    down_weight = dequantize(down_payload, down_scale)
    up_weight = dequantize(up_payload, up_scale)
    activated, gelu_slope = gelu_terms(pre_act)
    activated = activated.astype(BF16)

    other, own = hidden_partial(grad_pieces, down_weight)
    chip = own + swap_cores(other).astype(F32)
    hidden_grad = chip[:128]
    for step in (1, 2, 3):
        sent = chip[step * 128 : (step + 1) * 128].astype(BF16)
        hidden_grad = hidden_grad + from_y(sent, -step).astype(F32)
    gated_grad = (gelu_slope * hidden_grad).astype(BF16)

    gated_mine, gated_theirs = gather_y(gated_grad)
    parts = input_partial(gated_mine, gated_theirs, up_weight)
    rest = parts[0]
    for step in (1, 2, 3):
        rest = rest + from_grid(parts[step], True, -step).astype(F32)
    input_grad = rest[:64]
    for step in (1, 2, 3):
        sent = rest[step * 64 : (step + 1) * 64].astype(BF16)
        input_grad = input_grad + from_grid(sent, False, -step).astype(F32)
    input_grad = input_grad.astype(BF16)

    act_mine, act_theirs = gather_y(activated)
    down_grad = down_gradient(act_mine, act_theirs, grad_pieces)
    up_grad = up_gradient(gated_mine, gated_theirs, gather_grid(inputs))
    return (input_grad, up_grad, down_grad)


def solution(mesh):
    grid = Mesh(mesh.devices.reshape(4, 2, 4, 4), ("y", "k", "x", "z"))
    tokens, hidden = P(("x", "z"), ("y", "k")), P(("y", "k"), ("x", "z"))
    return jax.shard_map(
        per_device,
        mesh=grid,
        in_specs=(tokens, hidden, tokens, hidden, hidden, tokens, tokens),
        out_specs=(tokens, hidden, tokens),
        check_vma=False,
    )
```

```python
import jax
import jax.numpy as jnp
from jax import lax
from jax.experimental import pallas as pl
from jax.experimental.pallas import tpu as pltpu
from jax.sharding import Mesh
from jax.sharding import PartitionSpec as P

BF16, F32 = jnp.bfloat16, jnp.float32
TILE = 256


def dequantize(payload, scale):
    rows, cols = payload.shape
    blocks = payload.astype(F32).reshape(rows // 32, 32, cols)
    factor = jnp.exp2(scale.astype(F32))[:, None, :]
    return (blocks * factor).reshape(rows, cols).astype(BF16)


def gelu_terms(pre):
    values = pre.astype(F32)
    normal_cdf = 0.5 * (1.0 + jax.scipy.special.erf(values * 0.7071067811865476))
    activated = values * normal_cdf
    gelu_slope = normal_cdf + values * jnp.exp(-0.5 * values * values) * 0.3989422804014327
    return (activated, gelu_slope)


def shift_grid(first, step):
    pairs = []
    for k in range(2):
        for x in range(4):
            for z in range(4):
                along_x = (k == 0) == first
                to = (k, (x - step) % 4, z) if along_x else (k, x, (z - step) % 4)
                pairs.append((k * 16 + x * 4 + z, to[0] * 16 + to[1] * 4 + to[2]))
    return pairs


def from_grid(value, first, step):
    return lax.ppermute(value, ("k", "x", "z"), shift_grid(first, step))


def pair_y(value, step):
    pairs = []
    for y in range(4):
        for k in range(2):
            pairs.append((y * 2 + k, (y ^ (1 if (k == 0) == (step == 0) else 3)) * 2 + k))
    return lax.ppermute(value, ("y", "k"), pairs)


def pair_grid(value, step):
    pairs = []
    for k in range(2):
        for x in range(4):
            for z in range(4):
                flip = 3 if step % 2 else 1
                to = (x ^ flip, z) if (k == 0) == (step < 2) else (x, z ^ flip)
                pairs.append((k * 16 + x * 4 + z, k * 16 + to[0] * 4 + to[1]))
    return lax.ppermute(value, ("k", "x", "z"), pairs)


def swap_cores(value):
    return lax.ppermute(value, "k", [(0, 1), (1, 0)])


def gather_first(block):
    return jnp.concatenate([block] + [from_grid(block, True, step) for step in (1, 2, 3)])


def gather_second(stage):
    received = {step: from_grid(stage, False, step) for step in (2, 1, 3)}
    return [stage] + [received[step] for step in (1, 2, 3)]


def after(value, *others):
    return lax.optimization_barrier((value,) + others)[0]


FLIPS = (0, 1, 3, 2)


def place_of(x, z):
    k, y = lax.axis_index("k"), lax.axis_index("y")
    core, flip = z // 2, lax.bitwise_xor(x, y)
    near = jnp.where(core == 0, 3, 1)
    slot = jnp.where(flip == 0, 0, jnp.where(flip == 2, 3, jnp.where(flip == near, 1, 2)))
    return lax.rem(core + k, 2), slot * 2 + lax.rem(z, 2)


def grid_position(i, j):
    k, x, z = lax.axis_index("k"), lax.axis_index("x"), lax.axis_index("z")
    x = lax.rem(x + jnp.where(k == 0, i, j), 4)
    z = lax.rem(z + jnp.where(k == 0, j, i), 4)
    return x, z


def flipped_position(i, j):
    k, x, z = lax.axis_index("k"), lax.axis_index("x"), lax.axis_index("z")
    x = lax.bitwise_xor(x, jnp.where(k == 0, i, j))
    z = lax.bitwise_xor(z, jnp.where(k == 0, j, i))
    return x, z


NT = (((1,), (1,)), ((), ()))
TN = (((0,), (0,)), ((), ()))
WHOLE = pl.BlockSpec(memory_space=pltpu.VMEM)


def rows_at(start, count):
    return pl.ds(pl.multiple_of(start, 32), count)


def params(mib):
    return pltpu.CompilerParams(vmem_limit_bytes=mib * 1024 * 1024)


def cost(flops, moved):
    return pl.CostEstimate(flops=flops, bytes_accessed=moved, transcendentals=0)


def hidden_other_kernel(p0, p1, p2, p3, w, other, held):
    for j, piece in enumerate((p0, p1, p2, p3)):
        for i in range(4):
            half, place = place_of(*grid_position(i, j))
            held[rows_at(half * 512 + place * 64, 64)] = piece[i * 64 : (i + 1) * 64]

    @pl.loop(0, w.shape[0] // TILE, unroll=True)
    def _(n):
        columns = pl.ds(pl.multiple_of(n * TILE, TILE), TILE)
        out = lax.dot_general(held[512:], w[columns], NT, preferred_element_type=F32)
        other[:, columns] = out.astype(BF16)


def hidden_other(pieces, weight):
    n, depth = weight.shape
    return pl.pallas_call(
        hidden_other_kernel,
        out_shape=[jax.ShapeDtypeStruct((512, n), BF16), jax.ShapeDtypeStruct((1024, depth), BF16)],
        in_specs=[WHOLE] * 5,
        out_specs=[WHOLE] * 2,
        compiler_params=params(24),
        cost_estimate=cost(2 * 512 * n * depth, 2 * (1024 + n) * depth + 2 * 512 * n),
        name="hidden_other",
    )(*pieces, weight)


def hidden_own_kernel(held, w, own):
    @pl.loop(0, w.shape[0] // TILE, unroll=True)
    def _(n):
        columns = pl.ds(pl.multiple_of(n * TILE, TILE), TILE)
        own[:, columns] = lax.dot_general(held[:512], w[columns], NT, preferred_element_type=F32)


def hidden_own(ordered, weight):
    n, depth = weight.shape
    return pl.pallas_call(
        hidden_own_kernel,
        out_shape=jax.ShapeDtypeStruct((512, n), F32),
        in_specs=[WHOLE] * 2,
        out_specs=WHOLE,
        compiler_params=params(24),
        cost_estimate=cost(2 * 512 * n * depth, 2 * (1024 + n) * depth + 4 * 512 * n),
        name="hidden_own",
    )(ordered, weight)


def input_own_kernel(mine, w, own):
    @pl.loop(0, w.shape[0] // TILE, unroll=True)
    def _(n):
        columns = pl.ds(pl.multiple_of(n * TILE, TILE), TILE)
        own[:, columns] = lax.dot_general(mine[...], w[columns], NT, preferred_element_type=F32)


def input_own(mine, weight):
    n, depth = weight.shape
    return pl.pallas_call(
        input_own_kernel,
        out_shape=jax.ShapeDtypeStruct((512, n), F32),
        in_specs=[WHOLE] * 2,
        out_specs=WHOLE,
        compiler_params=params(24),
        cost_estimate=cost(2 * 512 * n * depth, 2 * (512 + n) * depth + 4 * 512 * n),
        name="input_own",
    )(mine, weight)


def input_all_kernel(theirs, w, own, o0, o1, o2, o3, both):
    @pl.loop(0, w.shape[0] // TILE, unroll=True)
    def _(n):
        columns = pl.ds(pl.multiple_of(n * TILE, TILE), TILE)
        both[:512] = own[:, columns]
        both[512:] = lax.dot_general(theirs[...], w[columns], NT, preferred_element_type=F32)
        for i, part in enumerate((o0, o1, o2, o3)):
            for j in range(4):
                half, place = place_of(*grid_position(i, j))
                part[pl.ds(j * 64, 64), columns] = both[rows_at(half * 512 + place * 64, 64)].astype(part.dtype)


def input_all(theirs, weight, own):
    n, depth = weight.shape
    return pl.pallas_call(
        input_all_kernel,
        out_shape=[jax.ShapeDtypeStruct((256, n), F32)] + [jax.ShapeDtypeStruct((256, n), BF16)] * 3,
        in_specs=[WHOLE] * 3,
        out_specs=[WHOLE] * 4,
        scratch_shapes=[pltpu.VMEM((1024, TILE), F32)],
        compiler_params=params(28),
        cost_estimate=cost(2 * 512 * n * depth, 2 * (512 + n) * depth + 4 * 1024 * n),
        name="input_all",
    )(theirs, weight, own)


def down_kernel(*refs):
    acts, (grad, out) = refs[:-2], refs[-2:]
    columns = pl.ds(pl.multiple_of(pl.program_id(0) * TILE, TILE), TILE)
    total, at = None, 0
    for act in acts:
        rows = slice(at, at + act.shape[0])
        part = lax.dot_general(act[:, columns], grad[rows], TN, preferred_element_type=F32)
        total = part if total is None else total + part
        at += act.shape[0]
    out[...] = total.astype(BF16)


def down_gradient(acts, grad):
    m, n = acts[0].shape[1], grad.shape[1]
    return pl.pallas_call(
        down_kernel,
        grid=(m // TILE,),
        out_shape=jax.ShapeDtypeStruct((m, n), BF16),
        in_specs=[WHOLE] * (len(acts) + 1),
        out_specs=pl.BlockSpec((TILE, n), lambda i: (i, 0)),
        compiler_params=params(24),
        cost_estimate=cost(2 * 1024 * n * m, 2 * 1024 * (n + m) + 2 * n * m),
        name="down_gradient",
    )(*acts, grad)


def up_kernel(mine, theirs, *rest):
    blocks, (out, held) = rest[:-2], rest[-2:]

    @pl.when(pl.program_id(0) == 0)
    def _():
        at = 0
        for block in blocks:
            for row in range(0, block.shape[0], 64):
                half, place = place_of(*flipped_position(FLIPS[at % 4], FLIPS[at // 4]))
                held[rows_at(half * 512 + place * 64, 64)] = block[row : row + 64]
                at += 1

    columns = pl.ds(pl.multiple_of(pl.program_id(0) * TILE, TILE), TILE)
    total = lax.dot_general(held[:512, columns], mine[...], TN, preferred_element_type=F32)
    total += lax.dot_general(held[512:, columns], theirs[...], TN, preferred_element_type=F32)
    out[...] = total.astype(BF16)


def up_gradient(mine, theirs, blocks):
    m, n = blocks[0].shape[1], mine.shape[1]
    return pl.pallas_call(
        up_kernel,
        grid=(m // TILE,),
        out_shape=jax.ShapeDtypeStruct((m, n), BF16),
        in_specs=[WHOLE] * (2 + len(blocks)),
        out_specs=pl.BlockSpec((TILE, n), lambda i: (i, 0)),
        scratch_shapes=[pltpu.VMEM((1024, m), BF16)],
        compiler_params=params(24),
        cost_estimate=cost(2 * 1024 * n * m, 2 * 1024 * (n + m) + 2 * n * m),
        name="up_gradient",
    )(mine, theirs, *blocks)


def together(*values):
    return lax.optimization_barrier(values)


def scatter_first(parts):
    rest = parts[0]
    received = {step: from_grid(parts[step], True, -step) for step in (2, 1, 3)}
    for step in (1, 2, 3):
        rest = rest + received[step].astype(F32)
    return rest


def scatter_second(rest):
    total, received = rest[:64], {}
    for step in (2, 1, 3):
        received[step] = from_grid(rest[step * 64 : (step + 1) * 64].astype(BF16), False, -step)
    for step in (1, 2, 3):
        total = total + received[step].astype(F32)
    return total.astype(BF16)


def per_device(inputs, pre_act, out_grad, up_payload, up_scale, down_payload, down_scale):
    down_weight = dequantize(down_payload, down_scale)
    up_weight = dequantize(up_payload, up_scale)
    activated, gelu_slope = gelu_terms(pre_act)
    activated = activated.astype(BF16)

    stage = gather_first(out_grad)
    pieces = gather_second(stage)
    act0, inputs = after(activated, stage), after(inputs, stage)
    act1 = pair_y(act0, 1)
    act2, act3 = pair_y(act0, 0), pair_y(act1, 0)
    in0 = jnp.concatenate([inputs, pair_grid(inputs, 0)])
    pieces[1], in0, act1, act2, act3, up_weight = together(pieces[1], in0, act1, act2, act3, up_weight)
    other, ordered = hidden_other(pieces, down_weight)
    chip = hidden_own(ordered, down_weight) + swap_cores(other).astype(F32)
    onward = chip[128:256] + pair_y(chip[384:].astype(BF16), 0).astype(F32)
    in0 = after(in0, chip)
    onward, in2, in1 = together(onward, pair_grid(in0, 2), pair_grid(in0, 1))
    hidden_grad = chip[:128] + pair_y(chip[256:384].astype(BF16), 0).astype(F32)
    hidden_grad = hidden_grad + pair_y(onward.astype(BF16), 1).astype(F32)
    hidden_grad, in3, in4 = together(hidden_grad, pair_grid(in1, 2), pair_grid(after(in0, onward), 3))
    gated = (gelu_slope * hidden_grad).astype(BF16)
    near, in5 = together(pair_y(gated, 1), pair_grid(after(in1, hidden_grad), 3))
    act = jnp.concatenate([act0, act1, act2, act3])
    mine = jnp.concatenate([gated, near, pair_y(gated, 0), pair_y(near, 0)])
    mine, in6, act_theirs = together(mine, pair_grid(after(in2, near), 3), swap_cores(act))
    theirs = swap_cores(mine)
    parts = list(input_all(theirs, up_weight, input_own(mine, up_weight)))
    parts[0], in7 = together(parts[0], pair_grid(after(in3, mine), 3))
    rest = scatter_first(parts)

    up_grad = up_gradient(mine, theirs, [in0, in1, in2, in3, in4, in5, in6, in7])
    rest, up_grad = together(rest, up_grad)
    down_grad = down_gradient([act, act_theirs], ordered)
    return (scatter_second(rest), up_grad, down_grad)


def solution(mesh):
    grid = Mesh(mesh.devices.reshape(4, 2, 4, 4), ("y", "k", "x", "z"))
    tokens, hidden = P(("x", "z"), ("y", "k")), P(("y", "k"), ("x", "z"))
    return jax.shard_map(
        per_device,
        mesh=grid,
        in_specs=(tokens, hidden, tokens, hidden, hidden, tokens, tokens),
        out_specs=(tokens, hidden, tokens),
        check_vma=False,
    )
```

```python
import jax
import jax.numpy as jnp
from jax import lax
from jax.experimental import pallas as pl
from jax.experimental.pallas import tpu as pltpu
from jax.sharding import Mesh
from jax.sharding import PartitionSpec as P

BF16, F32 = jnp.bfloat16, jnp.float32
TILE = 256


def dequantize(payload, scale):
    rows, cols = payload.shape
    blocks = payload.astype(F32).reshape(rows // 32, 32, cols)
    factor = jnp.exp2(scale.astype(F32))[:, None, :]
    return (blocks * factor).reshape(rows, cols).astype(BF16)


def gelu_terms(pre):
    values = pre.astype(F32)
    normal_cdf = 0.5 * (1.0 + jax.scipy.special.erf(values * 0.7071067811865476))
    activated = values * normal_cdf
    gelu_slope = normal_cdf + values * jnp.exp(-0.5 * values * values) * 0.3989422804014327
    return (activated, gelu_slope)


def shift_grid(first, step):
    pairs = []
    for k in range(2):
        for x in range(4):
            for z in range(4):
                along_x = (k == 0) == first
                to = (k, (x - step) % 4, z) if along_x else (k, x, (z - step) % 4)
                pairs.append((k * 16 + x * 4 + z, to[0] * 16 + to[1] * 4 + to[2]))
    return pairs


def from_grid(value, first, step):
    return lax.ppermute(value, ("k", "x", "z"), shift_grid(first, step))


def pair_y(value, step):
    pairs = []
    for y in range(4):
        for k in range(2):
            pairs.append((y * 2 + k, (y ^ (1 if (k == 0) == (step == 0) else 3)) * 2 + k))
    return lax.ppermute(value, ("y", "k"), pairs)


def pair_grid(value, step):
    pairs = []
    for k in range(2):
        for x in range(4):
            for z in range(4):
                flip = 3 if step % 2 else 1
                to = (x ^ flip, z) if (k == 0) == (step < 2) else (x, z ^ flip)
                pairs.append((k * 16 + x * 4 + z, k * 16 + to[0] * 4 + to[1]))
    return lax.ppermute(value, ("k", "x", "z"), pairs)


def swap_cores(value):
    return lax.ppermute(value, "k", [(0, 1), (1, 0)])


def gather_first(block):
    return jnp.concatenate([block] + [from_grid(block, True, step) for step in (1, 2, 3)])


def gather_second(stage):
    received = {step: from_grid(stage, False, step) for step in (2, 1, 3)}
    return [stage] + [received[step] for step in (1, 2, 3)]


def after(value, *others):
    return lax.optimization_barrier((value,) + others)[0]


FLIPS = (0, 1, 3, 2)


def place_of(x, z):
    k, y = lax.axis_index("k"), lax.axis_index("y")
    core, flip = z // 2, lax.bitwise_xor(x, y)
    near = jnp.where(core == 0, 3, 1)
    slot = jnp.where(flip == 0, 0, jnp.where(flip == 2, 3, jnp.where(flip == near, 1, 2)))
    return lax.rem(core + k, 2), slot * 2 + lax.rem(z, 2)


def grid_position(i, j):
    k, x, z = lax.axis_index("k"), lax.axis_index("x"), lax.axis_index("z")
    x = lax.rem(x + jnp.where(k == 0, i, j), 4)
    z = lax.rem(z + jnp.where(k == 0, j, i), 4)
    return x, z


def flipped_position(i, j):
    k, x, z = lax.axis_index("k"), lax.axis_index("x"), lax.axis_index("z")
    x = lax.bitwise_xor(x, jnp.where(k == 0, i, j))
    z = lax.bitwise_xor(z, jnp.where(k == 0, j, i))
    return x, z


NT = (((1,), (1,)), ((), ()))
TN = (((0,), (0,)), ((), ()))
WHOLE = pl.BlockSpec(memory_space=pltpu.VMEM)


def rows_at(start, count):
    return pl.ds(pl.multiple_of(start, 32), count)


def params(mib):
    return pltpu.CompilerParams(vmem_limit_bytes=mib * 1024 * 1024)


def cost(flops, moved):
    return pl.CostEstimate(flops=flops, bytes_accessed=moved, transcendentals=0)


def hidden_other_kernel(p0, p1, p2, p3, w, other, held):
    for j, piece in enumerate((p0, p1, p2, p3)):
        for i in range(4):
            half, place = place_of(*grid_position(i, j))
            held[rows_at(half * 512 + place * 64, 64)] = piece[i * 64 : (i + 1) * 64]

    @pl.loop(0, w.shape[0] // TILE, unroll=True)
    def _(n):
        columns = pl.ds(pl.multiple_of(n * TILE, TILE), TILE)
        out = lax.dot_general(held[512:], w[columns], NT, preferred_element_type=F32)
        other[:, columns] = out.astype(BF16)


def hidden_other(pieces, weight):
    n, depth = weight.shape
    return pl.pallas_call(
        hidden_other_kernel,
        out_shape=[jax.ShapeDtypeStruct((512, n), BF16), jax.ShapeDtypeStruct((1024, depth), BF16)],
        in_specs=[WHOLE] * 5,
        out_specs=[WHOLE] * 2,
        compiler_params=params(24),
        cost_estimate=cost(2 * 512 * n * depth, 2 * (1024 + n) * depth + 2 * 512 * n),
        name="hidden_other",
    )(*pieces, weight)


def hidden_own_kernel(held, w, own):
    @pl.loop(0, w.shape[0] // TILE, unroll=True)
    def _(n):
        columns = pl.ds(pl.multiple_of(n * TILE, TILE), TILE)
        own[:, columns] = lax.dot_general(held[:512], w[columns], NT, preferred_element_type=F32)


def hidden_own(ordered, weight):
    n, depth = weight.shape
    return pl.pallas_call(
        hidden_own_kernel,
        out_shape=jax.ShapeDtypeStruct((512, n), F32),
        in_specs=[WHOLE] * 2,
        out_specs=WHOLE,
        compiler_params=params(24),
        cost_estimate=cost(2 * 512 * n * depth, 2 * (1024 + n) * depth + 4 * 512 * n),
        name="hidden_own",
    )(ordered, weight)


def input_own_kernel(mine, w, own):
    @pl.loop(0, w.shape[0] // TILE, unroll=True)
    def _(n):
        columns = pl.ds(pl.multiple_of(n * TILE, TILE), TILE)
        own[:, columns] = lax.dot_general(mine[...], w[columns], NT, preferred_element_type=F32)


def input_own(mine, weight):
    n, depth = weight.shape
    return pl.pallas_call(
        input_own_kernel,
        out_shape=jax.ShapeDtypeStruct((512, n), F32),
        in_specs=[WHOLE] * 2,
        out_specs=WHOLE,
        compiler_params=params(24),
        cost_estimate=cost(2 * 512 * n * depth, 2 * (512 + n) * depth + 4 * 512 * n),
        name="input_own",
    )(mine, weight)


def input_all_kernel(theirs, w, own, o0, o1, o2, o3, both):
    @pl.loop(0, w.shape[0] // TILE, unroll=True)
    def _(n):
        columns = pl.ds(pl.multiple_of(n * TILE, TILE), TILE)
        both[:512] = own[:, columns]
        both[512:] = lax.dot_general(theirs[...], w[columns], NT, preferred_element_type=F32)
        for i, part in enumerate((o0, o1, o2, o3)):
            for j in range(4):
                half, place = place_of(*grid_position(i, j))
                part[pl.ds(j * 64, 64), columns] = both[rows_at(half * 512 + place * 64, 64)].astype(part.dtype)


def input_all(theirs, weight, own):
    n, depth = weight.shape
    return pl.pallas_call(
        input_all_kernel,
        out_shape=[jax.ShapeDtypeStruct((256, n), F32)] + [jax.ShapeDtypeStruct((256, n), BF16)] * 3,
        in_specs=[WHOLE] * 3,
        out_specs=[WHOLE] * 4,
        scratch_shapes=[pltpu.VMEM((1024, TILE), F32)],
        compiler_params=params(28),
        cost_estimate=cost(2 * 512 * n * depth, 2 * (512 + n) * depth + 4 * 1024 * n),
        name="input_all",
    )(theirs, weight, own)


def down_kernel(*refs):
    acts, (grad, out) = refs[:-2], refs[-2:]
    columns = pl.ds(pl.multiple_of(pl.program_id(0) * TILE, TILE), TILE)
    total, at = None, 0
    for act in acts:
        rows = slice(at, at + act.shape[0])
        part = lax.dot_general(act[:, columns], grad[rows], TN, preferred_element_type=F32)
        total = part if total is None else total + part
        at += act.shape[0]
    out[...] = total.astype(BF16)


def down_gradient(acts, grad):
    m, n = acts[0].shape[1], grad.shape[1]
    return pl.pallas_call(
        down_kernel,
        grid=(m // TILE,),
        out_shape=jax.ShapeDtypeStruct((m, n), BF16),
        in_specs=[WHOLE] * (len(acts) + 1),
        out_specs=pl.BlockSpec((TILE, n), lambda i: (i, 0)),
        compiler_params=params(24),
        cost_estimate=cost(2 * 1024 * n * m, 2 * 1024 * (n + m) + 2 * n * m),
        name="down_gradient",
    )(*acts, grad)


def up_kernel(mine, theirs, *rest):
    blocks, (out, held) = rest[:-2], rest[-2:]

    @pl.when(pl.program_id(0) == 0)
    def _():
        at = 0
        for block in blocks:
            for row in range(0, block.shape[0], 64):
                half, place = place_of(*flipped_position(FLIPS[at % 4], FLIPS[at // 4]))
                held[rows_at(half * 512 + place * 64, 64)] = block[row : row + 64]
                at += 1

    columns = pl.ds(pl.multiple_of(pl.program_id(0) * TILE, TILE), TILE)
    total = lax.dot_general(held[:512, columns], mine[...], TN, preferred_element_type=F32)
    total += lax.dot_general(held[512:, columns], theirs[...], TN, preferred_element_type=F32)
    out[...] = total.astype(BF16)


def up_gradient(mine, theirs, blocks):
    m, n = blocks[0].shape[1], mine.shape[1]
    return pl.pallas_call(
        up_kernel,
        grid=(m // TILE,),
        out_shape=jax.ShapeDtypeStruct((m, n), BF16),
        in_specs=[WHOLE] * (2 + len(blocks)),
        out_specs=pl.BlockSpec((TILE, n), lambda i: (i, 0)),
        scratch_shapes=[pltpu.VMEM((1024, m), BF16)],
        compiler_params=params(24),
        cost_estimate=cost(2 * 1024 * n * m, 2 * 1024 * (n + m) + 2 * n * m),
        name="up_gradient",
    )(mine, theirs, *blocks)


def together(*values):
    return lax.optimization_barrier(values)


def scatter_first(parts):
    rest = parts[0]
    received = {step: from_grid(parts[step], True, -step) for step in (2, 1, 3)}
    for step in (1, 2, 3):
        rest = rest + received[step].astype(F32)
    return rest


def scatter_second(rest):
    total, received = rest[:64], {}
    for step in (2, 1, 3):
        received[step] = from_grid(rest[step * 64 : (step + 1) * 64].astype(BF16), False, -step)
    for step in (1, 2, 3):
        total = total + received[step].astype(F32)
    return total.astype(BF16)


def per_device(inputs, pre_act, out_grad, up_payload, up_scale, down_payload, down_scale):
    down_weight = dequantize(down_payload, down_scale)
    up_weight = dequantize(up_payload, up_scale)
    activated, gelu_slope = gelu_terms(pre_act)
    activated = activated.astype(BF16)

    stage = gather_first(out_grad)
    pieces = gather_second(stage)
    act0, inputs = after(activated, stage), after(inputs, stage)
    act1 = pair_y(act0, 1)
    act2, act3 = pair_y(act0, 0), pair_y(act1, 0)
    in0 = jnp.concatenate([inputs, pair_grid(inputs, 0)])
    pieces[1], in0, act1, act2, act3, up_weight = together(pieces[1], in0, act1, act2, act3, up_weight)
    other, ordered = hidden_other(pieces, down_weight)
    chip = hidden_own(ordered, down_weight) + swap_cores(other).astype(F32)
    onward = chip[128:256] + pair_y(chip[384:].astype(BF16), 0).astype(F32)
    onward, in1 = together(onward, pair_grid(after(in0, chip), 1))
    hidden_grad = chip[:128] + pair_y(chip[256:384].astype(BF16), 0).astype(F32)
    hidden_grad = hidden_grad + pair_y(onward.astype(BF16), 1).astype(F32)

    gated = (gelu_slope * hidden_grad).astype(BF16)
    in01 = jnp.concatenate([in0, in1])
    near, in2, in3 = together(pair_y(gated, 1), pair_grid(in01, 2), pair_grid(in01, 3))
    act = after(jnp.concatenate([act0, act1, act2, act3]), onward)
    mine = jnp.concatenate([gated, near, pair_y(gated, 0), pair_y(near, 0)])
    mine, act_theirs = together(mine, swap_cores(act))

    theirs, in4 = swap_cores(mine), pair_grid(in2, 3)
    parts = list(input_all(theirs, up_weight, input_own(mine, up_weight)))
    rest = scatter_first(parts)

    act, in01 = after(act, parts[0]), after(in01, parts[0])
    down_grad = down_gradient([act, act_theirs], ordered)
    up_grad = up_gradient(mine, theirs, [in01, in2, in3, in4])
    rest, down_grad, up_grad = together(rest, down_grad, up_grad)
    return (scatter_second(rest), up_grad, down_grad)


def solution(mesh):
    grid = Mesh(mesh.devices.reshape(4, 2, 4, 4), ("y", "k", "x", "z"))
    tokens, hidden = P(("x", "z"), ("y", "k")), P(("y", "k"), ("x", "z"))
    return jax.shard_map(
        per_device,
        mesh=grid,
        in_specs=(tokens, hidden, tokens, hidden, hidden, tokens, tokens),
        out_specs=(tokens, hidden, tokens),
        check_vma=False,
    )
```

```python
import jax
import jax.numpy as jnp
from jax import lax
from jax.experimental import pallas as pl
from jax.experimental.pallas import tpu as pltpu
from jax.sharding import Mesh
from jax.sharding import PartitionSpec as P

BF16, F32 = jnp.bfloat16, jnp.float32
TILE = 256


def dequantize(payload, scale):
    rows, cols = payload.shape
    blocks = payload.astype(F32).reshape(rows // 32, 32, cols)
    factor = jnp.exp2(scale.astype(F32))[:, None, :]
    return (blocks * factor).reshape(rows, cols).astype(BF16)


def gelu_terms(pre):
    values = pre.astype(F32)
    normal_cdf = 0.5 * (1.0 + jax.scipy.special.erf(values * 0.7071067811865476))
    activated = values * normal_cdf
    gelu_slope = normal_cdf + values * jnp.exp(-0.5 * values * values) * 0.3989422804014327
    return (activated, gelu_slope)


def shift_grid(first, step):
    pairs = []
    for k in range(2):
        for x in range(4):
            for z in range(4):
                along_x = (k == 0) == first
                to = (k, (x - step) % 4, z) if along_x else (k, x, (z - step) % 4)
                pairs.append((k * 16 + x * 4 + z, to[0] * 16 + to[1] * 4 + to[2]))
    return pairs


def from_grid(value, first, step):
    return lax.ppermute(value, ("k", "x", "z"), shift_grid(first, step))


def pair_y(value, step):
    pairs = []
    for y in range(4):
        for k in range(2):
            pairs.append((y * 2 + k, (y ^ (1 if (k == 0) == (step == 0) else 3)) * 2 + k))
    return lax.ppermute(value, ("y", "k"), pairs)


def pair_grid(value, step):
    pairs = []
    for k in range(2):
        for x in range(4):
            for z in range(4):
                flip = 3 if step % 2 else 1
                to = (x ^ flip, z) if (k == 0) == (step < 2) else (x, z ^ flip)
                pairs.append((k * 16 + x * 4 + z, k * 16 + to[0] * 4 + to[1]))
    return lax.ppermute(value, ("k", "x", "z"), pairs)


def swap_cores(value):
    return lax.ppermute(value, "k", [(0, 1), (1, 0)])


def gather_first(block):
    return jnp.concatenate([block] + [from_grid(block, True, step) for step in (1, 2, 3)])


def gather_second(stage):
    received = {step: from_grid(stage, False, step) for step in (2, 1, 3)}
    return [stage] + [received[step] for step in (1, 2, 3)]


def after(value, *others):
    return lax.optimization_barrier((value,) + others)[0]


FLIPS = (0, 1, 3, 2)


def place_of(x, z):
    k, y = lax.axis_index("k"), lax.axis_index("y")
    core, flip = z // 2, lax.bitwise_xor(x, y)
    near = jnp.where(core == 0, 3, 1)
    slot = jnp.where(flip == 0, 0, jnp.where(flip == 2, 3, jnp.where(flip == near, 1, 2)))
    return lax.rem(core + k, 2), slot * 2 + lax.rem(z, 2)


def grid_position(i, j):
    k, x, z = lax.axis_index("k"), lax.axis_index("x"), lax.axis_index("z")
    x = lax.rem(x + jnp.where(k == 0, i, j), 4)
    z = lax.rem(z + jnp.where(k == 0, j, i), 4)
    return x, z


def flipped_position(i, j):
    k, x, z = lax.axis_index("k"), lax.axis_index("x"), lax.axis_index("z")
    x = lax.bitwise_xor(x, jnp.where(k == 0, i, j))
    z = lax.bitwise_xor(z, jnp.where(k == 0, j, i))
    return x, z


NT = (((1,), (1,)), ((), ()))
TN = (((0,), (0,)), ((), ()))
WHOLE = pl.BlockSpec(memory_space=pltpu.VMEM)


def rows_at(start, count):
    return pl.ds(pl.multiple_of(start, 32), count)


def params(mib):
    return pltpu.CompilerParams(vmem_limit_bytes=mib * 1024 * 1024)


def cost(flops, moved):
    return pl.CostEstimate(flops=flops, bytes_accessed=moved, transcendentals=0)


def hidden_other_kernel(p0, p1, p2, p3, w, other, held):
    for j, piece in enumerate((p0, p1, p2, p3)):
        for i in range(4):
            half, place = place_of(*grid_position(i, j))
            held[rows_at(half * 512 + place * 64, 64)] = piece[i * 64 : (i + 1) * 64]

    @pl.loop(0, w.shape[0] // TILE, unroll=True)
    def _(n):
        columns = pl.ds(pl.multiple_of(n * TILE, TILE), TILE)
        out = lax.dot_general(held[768:], w[columns], NT, preferred_element_type=F32)
        other[:, columns] = out.astype(BF16)


def hidden_other(pieces, weight):
    n, depth = weight.shape
    return pl.pallas_call(
        hidden_other_kernel,
        out_shape=[jax.ShapeDtypeStruct((256, n), BF16), jax.ShapeDtypeStruct((1024, depth), BF16)],
        in_specs=[WHOLE] * 5,
        out_specs=[WHOLE] * 2,
        compiler_params=params(24),
        cost_estimate=cost(2 * 512 * n * depth, 2 * (1024 + n) * depth + 2 * 512 * n),
        name="hidden_other",
    )(*pieces, weight)


def hidden_own_kernel(held, w, own):
    @pl.loop(0, w.shape[0] // TILE, unroll=True)
    def _(n):
        columns = pl.ds(pl.multiple_of(n * TILE, TILE), TILE)
        own[:, columns] = lax.dot_general(held[256:512], w[columns], NT, preferred_element_type=F32)


def hidden_own(ordered, weight):
    n, depth = weight.shape
    return pl.pallas_call(
        hidden_own_kernel,
        out_shape=jax.ShapeDtypeStruct((256, n), F32),
        in_specs=[WHOLE] * 2,
        out_specs=WHOLE,
        compiler_params=params(24),
        cost_estimate=cost(2 * 256 * n * depth, 2 * (1024 + n) * depth + 4 * 256 * n),
        name="hidden_own",
    )(ordered, weight)


def hidden_first_kernel(held, w, other, own, rows):
    rows[:256] = held[:256]
    rows[256:] = held[512:768]

    @pl.loop(0, w.shape[0] // TILE, unroll=True)
    def _(n):
        columns = pl.ds(pl.multiple_of(n * TILE, TILE), TILE)
        out = lax.dot_general(rows[...], w[columns], NT, preferred_element_type=F32)
        own[:, columns] = out[:256]
        other[:, columns] = out[256:].astype(BF16)


def hidden_first(ordered, weight):
    n, depth = weight.shape
    return pl.pallas_call(
        hidden_first_kernel,
        out_shape=[jax.ShapeDtypeStruct((256, n), BF16), jax.ShapeDtypeStruct((256, n), F32)],
        in_specs=[WHOLE] * 2,
        out_specs=[WHOLE] * 2,
        scratch_shapes=[pltpu.VMEM((512, depth), BF16)],
        compiler_params=params(24),
        cost_estimate=cost(2 * 512 * n * depth, 2 * (1024 + n) * depth + 6 * 256 * n),
        name="hidden_first",
    )(ordered, weight)


def input_own_kernel(mine, w, own):
    @pl.loop(0, w.shape[0] // TILE, unroll=True)
    def _(n):
        columns = pl.ds(pl.multiple_of(n * TILE, TILE), TILE)
        own[:, columns] = lax.dot_general(mine[...], w[columns], NT, preferred_element_type=F32)


def input_own(mine, weight):
    n, depth = weight.shape
    return pl.pallas_call(
        input_own_kernel,
        out_shape=jax.ShapeDtypeStruct((512, n), F32),
        in_specs=[WHOLE] * 2,
        out_specs=WHOLE,
        compiler_params=params(24),
        cost_estimate=cost(2 * 512 * n * depth, 2 * (512 + n) * depth + 4 * 512 * n),
        name="input_own",
    )(mine, weight)


def input_all_kernel(theirs, w, own, o0, o1, o2, o3, both):
    @pl.loop(0, w.shape[0] // TILE, unroll=True)
    def _(n):
        columns = pl.ds(pl.multiple_of(n * TILE, TILE), TILE)
        both[:512] = own[:, columns]
        both[512:] = lax.dot_general(theirs[...], w[columns], NT, preferred_element_type=F32)
        for i, part in enumerate((o0, o1, o2, o3)):
            for j in range(4):
                half, place = place_of(*grid_position(i, j))
                part[pl.ds(j * 64, 64), columns] = both[rows_at(half * 512 + place * 64, 64)].astype(part.dtype)


def input_all(theirs, weight, own):
    n, depth = weight.shape
    return pl.pallas_call(
        input_all_kernel,
        out_shape=[jax.ShapeDtypeStruct((256, n), F32)] + [jax.ShapeDtypeStruct((256, n), BF16)] * 3,
        in_specs=[WHOLE] * 3,
        out_specs=[WHOLE] * 4,
        scratch_shapes=[pltpu.VMEM((1024, TILE), F32)],
        compiler_params=params(28),
        cost_estimate=cost(2 * 512 * n * depth, 2 * (512 + n) * depth + 4 * 1024 * n),
        name="input_all",
    )(theirs, weight, own)


def down_kernel(*refs):
    acts, (grad, out) = refs[:-2], refs[-2:]
    columns = pl.ds(pl.multiple_of(pl.program_id(0) * TILE, TILE), TILE)
    total, at = None, 0
    for act in acts:
        rows = slice(at, at + act.shape[0])
        part = lax.dot_general(act[:, columns], grad[rows], TN, preferred_element_type=F32)
        total = part if total is None else total + part
        at += act.shape[0]
    out[...] = total.astype(BF16)


def down_gradient(acts, grad):
    m, n = acts[0].shape[1], grad.shape[1]
    return pl.pallas_call(
        down_kernel,
        grid=(m // TILE,),
        out_shape=jax.ShapeDtypeStruct((m, n), BF16),
        in_specs=[WHOLE] * (len(acts) + 1),
        out_specs=pl.BlockSpec((TILE, n), lambda i: (i, 0)),
        compiler_params=params(24),
        cost_estimate=cost(2 * 1024 * n * m, 2 * 1024 * (n + m) + 2 * n * m),
        name="down_gradient",
    )(*acts, grad)


def up_kernel(mine, theirs, *rest):
    blocks, (out, held) = rest[:-2], rest[-2:]

    @pl.when(pl.program_id(0) == 0)
    def _():
        at = 0
        for block in blocks:
            for row in range(0, block.shape[0], 64):
                half, place = place_of(*flipped_position(FLIPS[at % 4], FLIPS[at // 4]))
                held[rows_at(half * 512 + place * 64, 64)] = block[row : row + 64]
                at += 1

    columns = pl.ds(pl.multiple_of(pl.program_id(0) * TILE, TILE), TILE)
    total = lax.dot_general(held[:512, columns], mine[...], TN, preferred_element_type=F32)
    total += lax.dot_general(held[512:, columns], theirs[...], TN, preferred_element_type=F32)
    out[...] = total.astype(BF16)


def up_gradient(mine, theirs, blocks):
    m, n = blocks[0].shape[1], mine.shape[1]
    return pl.pallas_call(
        up_kernel,
        grid=(m // TILE,),
        out_shape=jax.ShapeDtypeStruct((m, n), BF16),
        in_specs=[WHOLE] * (2 + len(blocks)),
        out_specs=pl.BlockSpec((TILE, n), lambda i: (i, 0)),
        scratch_shapes=[pltpu.VMEM((1024, m), BF16)],
        compiler_params=params(24),
        cost_estimate=cost(2 * 1024 * n * m, 2 * 1024 * (n + m) + 2 * n * m),
        name="up_gradient",
    )(mine, theirs, *blocks)


def together(*values):
    return lax.optimization_barrier(values)


def scatter_first(parts):
    rest = parts[0]
    received = {step: from_grid(parts[step], True, -step) for step in (2, 1, 3)}
    for step in (1, 2, 3):
        rest = rest + received[step].astype(F32)
    return rest


def scatter_second(rest):
    total, received = rest[:64], {}
    for step in (2, 1, 3):
        received[step] = from_grid(rest[step * 64 : (step + 1) * 64].astype(BF16), False, -step)
    for step in (1, 2, 3):
        total = total + received[step].astype(F32)
    return total.astype(BF16)


def per_device(inputs, pre_act, out_grad, up_payload, up_scale, down_payload, down_scale):
    down_weight = dequantize(down_payload, down_scale)
    up_weight = dequantize(up_payload, up_scale)
    activated, gelu_slope = gelu_terms(pre_act)
    activated = activated.astype(BF16)

    stage = gather_first(out_grad)
    pieces = gather_second(stage)
    act0, inputs = after(activated, stage), after(inputs, stage)
    act1 = pair_y(act0, 1)
    act2, act3 = pair_y(act0, 0), pair_y(act1, 0)
    in0 = jnp.concatenate([inputs, pair_grid(inputs, 0)])
    pieces[1], in0, act1, act2, act3, up_weight = together(pieces[1], in0, act1, act2, act3, up_weight)
    other, ordered = hidden_other(pieces, down_weight)
    chip = hidden_own(ordered, down_weight) + swap_cores(other).astype(F32)
    far, last = pair_y(chip[128:].astype(BF16), 0), pair_y(chip[:128].astype(BF16), 0)
    other, own = hidden_first(after(ordered, chip), down_weight)
    first = own + swap_cores(other).astype(F32)
    onward = first[128:] + far.astype(F32)
    onward, in1 = together(onward, pair_grid(after(in0, chip), 1))
    hidden_grad = first[:128] + last.astype(F32)
    hidden_grad = hidden_grad + pair_y(onward.astype(BF16), 1).astype(F32)

    gated = (gelu_slope * hidden_grad).astype(BF16)
    in01 = jnp.concatenate([in0, in1])
    near, in2, in3 = together(pair_y(gated, 1), pair_grid(in01, 2), pair_grid(in01, 3))
    act = after(jnp.concatenate([act0, act1, act2, act3]), onward)
    mine = jnp.concatenate([gated, near, pair_y(gated, 0), pair_y(near, 0)])
    mine, act_theirs = together(mine, swap_cores(act))

    theirs, in4 = swap_cores(mine), pair_grid(in2, 3)
    parts = list(input_all(theirs, up_weight, input_own(mine, up_weight)))
    rest = scatter_first(parts)

    act, in01 = after(act, parts[0]), after(in01, parts[0])
    down_grad = down_gradient([act, act_theirs], ordered)
    up_grad = up_gradient(mine, theirs, [in01, in2, in3, in4])
    rest, down_grad, up_grad = together(rest, down_grad, up_grad)
    return (scatter_second(rest), up_grad, down_grad)


def solution(mesh):
    grid = Mesh(mesh.devices.reshape(4, 2, 4, 4), ("y", "k", "x", "z"))
    tokens, hidden = P(("x", "z"), ("y", "k")), P(("y", "k"), ("x", "z"))
    return jax.shard_map(
        per_device,
        mesh=grid,
        in_specs=(tokens, hidden, tokens, hidden, hidden, tokens, tokens),
        out_specs=(tokens, hidden, tokens),
        check_vma=False,
    )
```

```python
import jax
import jax.numpy as jnp
from jax import lax
from jax.experimental import pallas as pl
from jax.experimental.pallas import tpu as pltpu
from jax.sharding import Mesh
from jax.sharding import PartitionSpec as P

BF16, F32 = jnp.bfloat16, jnp.float32
TILE = 256


def dequantize(payload, scale):
    rows, cols = payload.shape
    blocks = payload.astype(F32).reshape(rows // 32, 32, cols)
    factor = jnp.exp2(scale.astype(F32))[:, None, :]
    return (blocks * factor).reshape(rows, cols).astype(BF16)


def gelu_terms(pre):
    values = pre.astype(F32)
    normal_cdf = 0.5 * (1.0 + jax.scipy.special.erf(values * 0.7071067811865476))
    activated = values * normal_cdf
    gelu_slope = normal_cdf + values * jnp.exp(-0.5 * values * values) * 0.3989422804014327
    return (activated, gelu_slope)


def shift_grid(first, step):
    pairs = []
    for k in range(2):
        for x in range(4):
            for z in range(4):
                along_x = (k == 0) == first
                to = (k, (x - step) % 4, z) if along_x else (k, x, (z - step) % 4)
                pairs.append((k * 16 + x * 4 + z, to[0] * 16 + to[1] * 4 + to[2]))
    return pairs


def from_grid(value, first, step):
    return lax.ppermute(value, ("k", "x", "z"), shift_grid(first, step))


def pair_y(value, step):
    pairs = []
    for y in range(4):
        for k in range(2):
            pairs.append((y * 2 + k, (y ^ (1 if (k == 0) == (step == 0) else 3)) * 2 + k))
    return lax.ppermute(value, ("y", "k"), pairs)


def pair_grid(value, step):
    pairs = []
    for k in range(2):
        for x in range(4):
            for z in range(4):
                flip = 3 if step % 2 else 1
                to = (x ^ flip, z) if (k == 0) == (step < 2) else (x, z ^ flip)
                pairs.append((k * 16 + x * 4 + z, k * 16 + to[0] * 4 + to[1]))
    return lax.ppermute(value, ("k", "x", "z"), pairs)


def swap_cores(value):
    return lax.ppermute(value, "k", [(0, 1), (1, 0)])


def gather_first(block):
    return jnp.concatenate([block] + [from_grid(block, True, step) for step in (1, 2, 3)])


def gather_second(stage):
    received = {step: from_grid(stage, False, step) for step in (3, 2, 1)}
    return [stage] + [received[step] for step in (1, 2, 3)]


def after(value, *others):
    return lax.optimization_barrier((value,) + others)[0]


FLIPS = (0, 1, 3, 2)


def place_of(x, z):
    k, y = lax.axis_index("k"), lax.axis_index("y")
    core, flip = z // 2, lax.bitwise_xor(x, y)
    near = jnp.where(core == 0, 3, 1)
    slot = jnp.where(flip == 0, 0, jnp.where(flip == 2, 3, jnp.where(flip == near, 1, 2)))
    return lax.rem(core + k, 2), slot * 2 + lax.rem(z, 2)


def grid_position(i, j):
    k, x, z = lax.axis_index("k"), lax.axis_index("x"), lax.axis_index("z")
    x = lax.rem(x + jnp.where(k == 0, i, j), 4)
    z = lax.rem(z + jnp.where(k == 0, j, i), 4)
    return x, z


def flipped_position(i, j):
    k, x, z = lax.axis_index("k"), lax.axis_index("x"), lax.axis_index("z")
    x = lax.bitwise_xor(x, jnp.where(k == 0, i, j))
    z = lax.bitwise_xor(z, jnp.where(k == 0, j, i))
    return x, z


NT = (((1,), (1,)), ((), ()))
TN = (((0,), (0,)), ((), ()))
WHOLE = pl.BlockSpec(memory_space=pltpu.VMEM)


def rows_at(start, count):
    return pl.ds(pl.multiple_of(start, 32), count)


def params(mib):
    return pltpu.CompilerParams(vmem_limit_bytes=mib * 1024 * 1024)


def cost(flops, moved):
    return pl.CostEstimate(flops=flops, bytes_accessed=moved, transcendentals=0)


def hidden_other_kernel(p0, p1, p2, p3, w, other, held):
    for j, piece in enumerate((p0, p1, p2, p3)):
        for i in range(4):
            half, place = place_of(*grid_position(i, j))
            held[rows_at(half * 512 + place * 64, 64)] = piece[i * 64 : (i + 1) * 64]

    @pl.loop(0, w.shape[0] // TILE, unroll=True)
    def _(n):
        columns = pl.ds(pl.multiple_of(n * TILE, TILE), TILE)
        out = lax.dot_general(held[768:], w[columns], NT, preferred_element_type=F32)
        other[:, columns] = out.astype(BF16)


def hidden_other(pieces, weight):
    n, depth = weight.shape
    return pl.pallas_call(
        hidden_other_kernel,
        out_shape=[jax.ShapeDtypeStruct((256, n), BF16), jax.ShapeDtypeStruct((1024, depth), BF16)],
        in_specs=[WHOLE] * 5,
        out_specs=[WHOLE] * 2,
        compiler_params=params(24),
        cost_estimate=cost(2 * 512 * n * depth, 2 * (1024 + n) * depth + 2 * 512 * n),
        name="hidden_other",
    )(*pieces, weight)


def hidden_own_kernel(held, w, own):
    @pl.loop(0, w.shape[0] // TILE, unroll=True)
    def _(n):
        columns = pl.ds(pl.multiple_of(n * TILE, TILE), TILE)
        own[:, columns] = lax.dot_general(held[256:512], w[columns], NT, preferred_element_type=F32)


def hidden_own(ordered, weight):
    n, depth = weight.shape
    return pl.pallas_call(
        hidden_own_kernel,
        out_shape=jax.ShapeDtypeStruct((256, n), F32),
        in_specs=[WHOLE] * 2,
        out_specs=WHOLE,
        compiler_params=params(24),
        cost_estimate=cost(2 * 256 * n * depth, 2 * (1024 + n) * depth + 4 * 256 * n),
        name="hidden_own",
    )(ordered, weight)


def hidden_first_kernel(held, w, other, own, rows):
    rows[:256] = held[:256]
    rows[256:] = held[512:768]

    @pl.loop(0, w.shape[0] // TILE, unroll=True)
    def _(n):
        columns = pl.ds(pl.multiple_of(n * TILE, TILE), TILE)
        out = lax.dot_general(rows[...], w[columns], NT, preferred_element_type=F32)
        own[:, columns] = out[:256]
        other[:, columns] = out[256:].astype(BF16)


def hidden_first(ordered, weight):
    n, depth = weight.shape
    return pl.pallas_call(
        hidden_first_kernel,
        out_shape=[jax.ShapeDtypeStruct((256, n), BF16), jax.ShapeDtypeStruct((256, n), F32)],
        in_specs=[WHOLE] * 2,
        out_specs=[WHOLE] * 2,
        scratch_shapes=[pltpu.VMEM((512, depth), BF16)],
        compiler_params=params(24),
        cost_estimate=cost(2 * 512 * n * depth, 2 * (1024 + n) * depth + 6 * 256 * n),
        name="hidden_first",
    )(ordered, weight)


def input_own_kernel(mine, w, own):
    @pl.loop(0, w.shape[0] // TILE, unroll=True)
    def _(n):
        columns = pl.ds(pl.multiple_of(n * TILE, TILE), TILE)
        own[:, columns] = lax.dot_general(mine[...], w[columns], NT, preferred_element_type=F32)


def input_own(mine, weight):
    n, depth = weight.shape
    return pl.pallas_call(
        input_own_kernel,
        out_shape=jax.ShapeDtypeStruct((512, n), F32),
        in_specs=[WHOLE] * 2,
        out_specs=WHOLE,
        compiler_params=params(24),
        cost_estimate=cost(2 * 512 * n * depth, 2 * (512 + n) * depth + 4 * 512 * n),
        name="input_own",
    )(mine, weight)


def input_all_kernel(theirs, w, own, o0, o1, o2, o3, both):
    @pl.loop(0, w.shape[0] // TILE, unroll=True)
    def _(n):
        columns = pl.ds(pl.multiple_of(n * TILE, TILE), TILE)
        both[:512] = own[:, columns]
        both[512:] = lax.dot_general(theirs[...], w[columns], NT, preferred_element_type=F32)
        for i, part in enumerate((o0, o1, o2, o3)):
            for j in range(4):
                half, place = place_of(*grid_position(i, j))
                part[pl.ds(j * 64, 64), columns] = both[rows_at(half * 512 + place * 64, 64)].astype(part.dtype)


def input_all(theirs, weight, own):
    n, depth = weight.shape
    return pl.pallas_call(
        input_all_kernel,
        out_shape=[jax.ShapeDtypeStruct((256, n), F32)] + [jax.ShapeDtypeStruct((256, n), BF16)] * 3,
        in_specs=[WHOLE] * 3,
        out_specs=[WHOLE] * 4,
        scratch_shapes=[pltpu.VMEM((1024, TILE), F32)],
        compiler_params=params(28),
        cost_estimate=cost(2 * 512 * n * depth, 2 * (512 + n) * depth + 4 * 1024 * n),
        name="input_all",
    )(theirs, weight, own)


def down_kernel(*refs):
    acts, (grad, out) = refs[:-2], refs[-2:]
    columns = pl.ds(pl.multiple_of(pl.program_id(0) * TILE, TILE), TILE)
    total, at = None, 0
    for act in acts:
        rows = slice(at, at + act.shape[0])
        part = lax.dot_general(act[:, columns], grad[rows], TN, preferred_element_type=F32)
        total = part if total is None else total + part
        at += act.shape[0]
    out[...] = total.astype(BF16)


def down_gradient(acts, grad):
    m, n = acts[0].shape[1], grad.shape[1]
    return pl.pallas_call(
        down_kernel,
        grid=(m // TILE,),
        out_shape=jax.ShapeDtypeStruct((m, n), BF16),
        in_specs=[WHOLE] * (len(acts) + 1),
        out_specs=pl.BlockSpec((TILE, n), lambda i: (i, 0)),
        compiler_params=params(24),
        cost_estimate=cost(2 * 1024 * n * m, 2 * 1024 * (n + m) + 2 * n * m),
        name="down_gradient",
    )(*acts, grad)


def up_kernel(mine, theirs, *rest):
    blocks, (out, held) = rest[:-2], rest[-2:]

    @pl.when(pl.program_id(0) == 0)
    def _():
        at = 0
        for block in blocks:
            for row in range(0, block.shape[0], 64):
                half, place = place_of(*flipped_position(FLIPS[at % 4], FLIPS[at // 4]))
                held[rows_at(half * 512 + place * 64, 64)] = block[row : row + 64]
                at += 1

    columns = pl.ds(pl.multiple_of(pl.program_id(0) * TILE, TILE), TILE)
    total = lax.dot_general(held[:512, columns], mine[...], TN, preferred_element_type=F32)
    total += lax.dot_general(held[512:, columns], theirs[...], TN, preferred_element_type=F32)
    out[...] = total.astype(BF16)


def up_gradient(mine, theirs, blocks):
    m, n = blocks[0].shape[1], mine.shape[1]
    return pl.pallas_call(
        up_kernel,
        grid=(m // TILE,),
        out_shape=jax.ShapeDtypeStruct((m, n), BF16),
        in_specs=[WHOLE] * (2 + len(blocks)),
        out_specs=pl.BlockSpec((TILE, n), lambda i: (i, 0)),
        scratch_shapes=[pltpu.VMEM((1024, m), BF16)],
        compiler_params=params(24),
        cost_estimate=cost(2 * 1024 * n * m, 2 * 1024 * (n + m) + 2 * n * m),
        name="up_gradient",
    )(mine, theirs, *blocks)


def together(*values):
    return lax.optimization_barrier(values)


def scatter_first(parts):
    rest = parts[0]
    received = {step: from_grid(parts[step], True, -step) for step in (2, 1, 3)}
    for step in (1, 2, 3):
        rest = rest + received[step].astype(F32)
    return rest


def scatter_second(rest):
    total, received = rest[:64], {}
    for step in (2, 1, 3):
        received[step] = from_grid(rest[step * 64 : (step + 1) * 64].astype(BF16), False, -step)
    for step in (1, 2, 3):
        total = total + received[step].astype(F32)
    return total.astype(BF16)


def per_device(inputs, pre_act, out_grad, up_payload, up_scale, down_payload, down_scale):
    down_weight = dequantize(down_payload, down_scale)
    up_weight = dequantize(up_payload, up_scale)
    activated, gelu_slope = gelu_terms(pre_act)
    activated = activated.astype(BF16)

    stage = gather_first(out_grad)
    pieces = gather_second(stage)
    act0, inputs = after(activated, stage), after(inputs, stage)
    act1 = pair_y(act0, 1)
    act2, act3 = pair_y(act0, 0), pair_y(act1, 0)
    in0 = jnp.concatenate([inputs, pair_grid(inputs, 0)])
    pieces[1], in0, act1, act2, act3, up_weight = together(pieces[1], in0, act1, act2, act3, up_weight)
    other, ordered = hidden_other(pieces, down_weight)
    chip = hidden_own(ordered, down_weight) + swap_cores(other).astype(F32)
    far, last = pair_y(chip[128:].astype(BF16), 0), pair_y(chip[:128].astype(BF16), 0)
    other, own = hidden_first(after(ordered, chip), down_weight)
    first = own + swap_cores(other).astype(F32)
    onward = first[128:] + far.astype(F32)
    onward, in1 = together(onward, pair_grid(after(in0, chip), 1))
    hidden_grad = first[:128] + last.astype(F32)
    hidden_grad = hidden_grad + pair_y(onward.astype(BF16), 1).astype(F32)

    gated = (gelu_slope * hidden_grad).astype(BF16)
    in01 = jnp.concatenate([in0, in1])
    near, in2, in3 = together(pair_y(gated, 1), pair_grid(in01, 2), pair_grid(in01, 3))
    act = after(jnp.concatenate([act0, act1, act2, act3]), onward)
    mine = jnp.concatenate([gated, near, pair_y(gated, 0), pair_y(near, 0)])
    mine, act_theirs = together(mine, swap_cores(act))

    theirs, in4 = swap_cores(mine), pair_grid(in2, 3)
    parts = list(input_all(theirs, up_weight, input_own(mine, up_weight)))
    rest = scatter_first(parts)

    act, in01 = after(act, parts[0]), after(in01, parts[0])
    down_grad = down_gradient([act, act_theirs], ordered)
    up_grad = up_gradient(mine, theirs, [in01, in2, in3, in4])
    rest, down_grad, up_grad = together(rest, down_grad, up_grad)
    return (scatter_second(rest), up_grad, down_grad)


def solution(mesh):
    grid = Mesh(mesh.devices.reshape(4, 2, 4, 4), ("y", "k", "x", "z"))
    tokens, hidden = P(("x", "z"), ("y", "k")), P(("y", "k"), ("x", "z"))
    return jax.shard_map(
        per_device,
        mesh=grid,
        in_specs=(tokens, hidden, tokens, hidden, hidden, tokens, tokens),
        out_specs=(tokens, hidden, tokens),
        check_vma=False,
    )
```
